32 devices in a mesh: ka: 16 (over z, y, core), ga: 2 (over x).
Axes of the slice: x: 2, y: 2, z: 4, core: 2. Of those that a mesh axis runs over, the one named last changes fastest.
Arguments:
- orbitals: bfloat16 [16, 16, 4096], P('ka', None, 'ga'), may hold values from -6 to 6
- interp_vectors: bfloat16 [4096, 4096], P(None, 'ga'), may hold values from -0.09375 to 0.09375
- screening: bfloat16 [9216, 4096], P('ka', 'ga'), may hold values from 0.049804688 to 2
- bare_coulomb: float32 [4096], P('ga'), may hold values from 0.05 to 2
- slab_kpoints: int32 [16], P('ka'), may hold values from 0 to 9215, as said below
Outputs:
- kernel: float32 [16, 7, 1, 4096], P('ka', None, None, 'ga')
The draws below stay inside these ranges and needn't reach their ends.
Inputs may be any that keep to these rules, and one draw needn't show every extreme that they name: `slab_kpoints`: distinct grid points, each written as ix * 96 + iy with ix and iy its two grid coordinates.
All inputs are finite; a program needn't handle non-finite values.
Results may differ from the reference program's by a relative error of at most 0.0049.
Values may be sent and summed in bfloat16 or wider, within the bound.
A program may use at most 128 MiB of HBM per device.

```python
import math
import jax
import jax.numpy as jnp

NV = 8
NC = 8
NG = 4096
NPTS = 4096
NKX = 96
KD = 1
RSTEPS = 3
NK = 9216
NOFF = 7
SLAB = 16
N_KA = 16


def draw_slab_kpoints(key, part):
    return jax.random.permutation(key, NK)[:SLAB].astype(jnp.int32)


def block_scale(stream_key, shape, cuts, least, largest):
    level = 1.0
    for dim, parts in cuts:
        draws = jax.random.uniform(jax.random.fold_in(jax.random.fold_in(stream_key, 6), dim), (parts,), jnp.float32, least / len(cuts), largest / len(cuts))
        level = level * jnp.repeat(jnp.exp(draws), shape[dim] // parts).reshape((-1,) + (1,) * (len(shape) - 1 - dim))
    return level


def gaussian(stream_key, extent, scale, reach, cuts=(), kind=jnp.bfloat16):
    gain = block_scale(stream_key, extent, cuts, -0.22, 0.18) if cuts else 1.0
    values = jax.random.normal(stream_key, extent, jnp.float32) * scale * gain
    return jnp.minimum(jnp.maximum(values, -reach), reach).astype(kind)


def setup_inputs(seed: int = 0) -> dict:
    key_list = jax.random.split(jax.random.key(seed), 6)
    orbitals = gaussian(key_list[0], (SLAB, NV + NC, NPTS), 1.0, 6.0, ((0, 16), (2, 2)))
    interp_vectors = gaussian(key_list[1], (NPTS, NG), NPTS ** -0.5, 0.09375, ((1, 2),))
    screening = jnp.clip(jnp.exp(math.log(2.0) - 3.6927934 * jax.random.uniform(key_list[2], (NK, NG), jnp.float32) ** block_scale(key_list[2], (NK, NG), ((0, 16), (1, 2)), -0.2, 0.2)), 0.049804688, 2.0).astype(jnp.bfloat16)
    bare_coulomb = jnp.clip(jnp.exp(math.log(2.0) - 3.6888794 * jax.random.uniform(key_list[3], (NG,), jnp.float32) ** block_scale(key_list[3], (NG,), ((0, 2),), -0.2, 0.2)), 0.05, 2.0)
    slab_kpoints = draw_slab_kpoints(jax.random.fold_in(key_list[5], 71), 0)
    return dict(orbitals=orbitals, interp_vectors=interp_vectors, screening=screening, bare_coulomb=bare_coulomb, slab_kpoints=slab_kpoints)


def band_products(first_set, second_set):
    product = first_set.astype(jnp.float32)[:, :, None, :, None, :] * second_set.astype(jnp.float32)[:, None, :, None, :, :]
    dims_in = product.shape
    return product.reshape(dims_in[0], dims_in[1], dims_in[2], dims_in[3] * dims_in[4], dims_in[5]).astype(jnp.bfloat16)


def project(points, interp_vectors):
    dims_in = points.shape
    flattened = points.reshape(-1, dims_in[-1])
    pair_waves = jnp.dot(flattened, interp_vectors, preferred_element_type=jnp.float32)
    return pair_waves.astype(jnp.bfloat16).reshape(dims_in[:-1] + (interp_vectors.shape[1],))


def momentum_index(first_point, second_point):
    row_step = (first_point // NKX - second_point // NKX) % NKX
    col_step = (first_point % NKX - second_point % NKX) % NKX
    return (row_step * NKX + col_step).astype(jnp.int32)


def reference(orbitals, interp_vectors, screening, bare_coulomb, slab_kpoints):
    blocks = orbitals.reshape(N_KA, KD, NV + NC, NPTS)
    valence = blocks[:, :, :NV]
    conduct = blocks[:, :, NV:]
    own_product = valence.astype(jnp.float32)[:, :, :, None, :] * conduct.astype(jnp.float32)[:, :, None, :, :]
    exchange_points = own_product.reshape(N_KA, KD, NV * NC, NPTS).astype(jnp.bfloat16)
    exchange_waves = project(exchange_points, interp_vectors)
    weighted_x = (exchange_waves.astype(jnp.float32) * bare_coulomb).astype(jnp.bfloat16)
    grid_points = slab_kpoints.reshape(N_KA, KD)
    pieces = []
    for offset in range(-RSTEPS, RSTEPS + 1):
        partner = jnp.roll(blocks, offset, axis=0)
        partner_ex = jnp.roll(exchange_waves, offset, axis=0)
        partner_k = jnp.roll(grid_points, offset, axis=0)
        cond_pairs = band_products(conduct, partner[:, :, NV:])
        vale_pairs = band_products(valence, partner[:, :, :NV])
        pair_waves = project(jnp.concatenate([cond_pairs, vale_pairs], axis=3), interp_vectors)
        momentum = momentum_index(grid_points[:, :, None], partner_k[:, None, :])
        screen_rows = screening[momentum].astype(jnp.float32)
        weighted = (pair_waves[:, :, :, :NC * NC].astype(jnp.float32) * screen_rows[:, :, :, None, :]).astype(jnp.bfloat16)
        direct = jnp.einsum('bklxg,bklyg->bklxy', weighted.astype(jnp.float32), pair_waves[:, :, :, NC * NC:].astype(jnp.float32))
        direct = direct.reshape(N_KA, KD, KD, NC, NC, NV, NV).transpose(0, 1, 2, 5, 3, 6, 4).reshape(N_KA, KD, KD, -1)
        exch_term = jnp.einsum('bkxg,blyg->bklxy', weighted_x.astype(jnp.float32), partner_ex.astype(jnp.float32))
        exch_term = exch_term.reshape(N_KA, KD, KD, -1)
        pieces.append(2.0 * exch_term - direct)
    kernel = jnp.stack(pieces, axis=2).reshape(SLAB, NOFF, KD, (NV * NC) ** 2)
    return kernel * (NG ** -0.5)
```

```python
import functools

import jax
import jax.numpy as jnp
from jax import lax
from jax.experimental import pallas as pl
from jax.experimental.pallas import tpu as pltpu
from jax.sharding import PartitionSpec as P

NV = 8
NC = 8
NG = 4096
NKX = 96
RSTEPS = 3
NP = NV * NC
TILE = 256
F32, BF16, I32 = jnp.float32, jnp.bfloat16, jnp.int32


def dot(a, b):
    return lax.dot_general(a, b, (((1,), (0,)), ((), ())), preferred_element_type=F32)


def dot_t(a, b):
    return lax.dot_general(a, b, (((1,), (1,)), ((), ())), preferred_element_type=F32)


def iota(shape, dim):
    return lax.broadcasted_iota(I32, shape, dim)


def flip(x, j, bits):
    for s in range(bits):
        if (j >> s) & 1:
            x = x + (1 << s) - 2 * (1 << s) * ((x // (1 << s)) % 2)
    return x


def reverse(i, bits):
    return sum(((i >> s) & 1) << (bits - 1 - s) for s in range(bits))


def onehot(cond):
    return jnp.where(cond, 1.0, 0.0).astype(BF16)


def kernel(
    n_ka, n_ga,
    orb, kpt, bare, interp, screening, out,
    slots, kall, table, pick, arrived, points, weights, waves, sbuf, rbuf,
    osend, orecv, ksend, krecv, tsem, isem, psend, precv, fsend, frecv,
):
    k, g = lax.axis_index("ka"), lax.axis_index("ga")
    bits = n_ka.bit_length() - 1
    steps = RSTEPS + 1
    half_pts = orb.shape[2]
    pts, cols = interp.shape
    tiles = cols // TILE
    rows_here = screening.shape[0]
    share = sbuf.shape[1] // n_ga

    def ka(x):
        return lax.rem(x + n_ka, n_ka)

    def ga(x):
        return lax.rem(x + n_ga, n_ga)

    def remote(src, dst, ss, rs, kk, gg):
        return pltpu.make_async_remote_copy(
            src_ref=src, dst_ref=dst, send_sem=ss, recv_sem=rs,
            device_id=(kk, gg), device_id_type=pl.DeviceIdType.MESH,
        )

    def load_tile(t):
        at = pl.ds(pl.multiple_of(t * TILE, TILE), TILE)
        return pltpu.make_async_copy(interp.at[:, at], weights.at[t], isem.at[t])

    barrier = pltpu.get_barrier_semaphore()
    peers = [(flip(k, j, bits), g) for j in range(1, n_ka)]
    peers += [(ka(k + d), ga(g + j)) for d in range(-RSTEPS, RSTEPS + 1) for j in range(1, n_ga)]
    for kk, gg in peers:
        pl.semaphore_signal(barrier, inc=1, device_id=(kk, gg), device_id_type=pl.DeviceIdType.MESH)
    table_copy = pltpu.make_async_copy(screening, table, tsem.at[0])
    table_copy.start()
    for t in range(tiles):
        load_tile(t).start()
    point = kpt[0]
    kall[k, 0] = jnp.full((8, 128), point // NKX, I32)
    kall[k, 1] = jnp.full((8, 128), point % NKX, I32)
    slots[0, g] = orb[0]
    pl.semaphore_wait(barrier, len(peers))

    def kpt_copy(j, owner):
        return remote(kall.at[owner], kall.at[owner], ksend.at[j], krecv.at[j], flip(k, j, bits), g)

    for j in range(1, n_ka):
        kpt_copy(j, k).start()
    moves = [(d, j) for d in range(steps) for j in range(n_ga) if d or j]

    def orb_copy(d, j, gg):
        return remote(
            orb.at[0], slots.at[d, gg], osend.at[d, j], orecv.at[d, j], ka(k + d), ga(g + j)
        )

    for d, j in moves:
        orb_copy(d, j, g).start()

    for j in range(1, n_ka):
        kpt_copy(j, flip(k, j, bits)).wait_recv()

    table_copy.wait()
    sub = iota((8, 128), 0)
    lane = iota((16, rows_here), 1)
    pieces = []
    for i in range(n_ka):
        dest = flip(k, reverse(i, bits), bits)
        dx, dy = kall[dest, 0], kall[dest, 1]
        want = jnp.zeros((8, 128), I32)
        for d in range(1, steps):
            other = ka(dest - d)
            x, y = dx - kall[other, 0], dy - kall[other, 1]
            there = jnp.where(x < 0, x + NKX, x) * NKX + jnp.where(y < 0, y + NKX, y)
            back = jnp.where(x > 0, NKX - x, -x) * NKX + jnp.where(y > 0, NKX - y, -y)
            want = jnp.where(sub == 2 * d - 1, there, want)
            want = jnp.where(sub == 2 * d, back, want)
        local = (want - k * rows_here)[:, :1]
        local = jnp.concatenate([local, local], axis=0)
        pieces.append(jnp.where(lane == local, 1.0, 0.0))
    picker = jnp.concatenate(pieces, axis=0).astype(BF16)
    half_cols = cols // 2
    picked = dot(picker, table[...])
    upper = (iota((n_ka * 16, half_cols), 0) // 8) % 2
    picked = jnp.where(upper == 0, picked[:, :half_cols], picked[:, half_cols:])
    pick[...] = picked.astype(BF16).reshape(n_ka, 16, half_cols)

    def pick_copy(s):
        half = n_ka >> (s + 1)
        return remote(
            pick.at[pl.ds(half, half)], arrived.at[pl.ds(half, half)],
            psend.at[s], precv.at[s], flip(k, 1 << s, bits), g,
        )

    def pick_step(s):
        half = n_ka >> (s + 1)
        pick_copy(s).wait_recv()
        pick[:half] = (pick[:half].astype(F32) + arrived[half:2 * half].astype(F32)).astype(BF16)
        if s + 1 < bits:
            pick_copy(s + 1).start()

    pick_copy(0).start()

    width = 512
    for d in range(steps):
        for j in range(n_ga):
            if d or j:
                orb_copy(d, j, ga(g - j)).wait_recv()

        def products(c, carry, d=d):
            h, off = c // (half_pts // width), c % (half_pts // width)
            at = pl.ds(pl.multiple_of(off * width, width), width)
            to = pl.ds(pl.multiple_of(c * width, width), width)
            own = slots[0, h, :, at].astype(F32)
            par = slots[d, h, :, at].astype(F32)
            own_v, own_c, par_v, par_c = own[:NV], own[NV:], par[:NV], par[NV:]
            ex = jnp.concatenate([par_v[i:i + 1] * par_c for i in range(NV)], axis=0)
            cond = jnp.concatenate([own_c[i:i + 1] * par_c for i in range(NC)], axis=0)
            vale = jnp.concatenate([par_v[i:i + 1] * own_v for i in range(NV)], axis=0)
            points[pl.ds(d * NP, NP), to] = ex.astype(BF16)
            points[pl.ds((steps + 2 * d) * NP, NP), to] = cond.astype(BF16)
            points[pl.ds((steps + 2 * d + 1) * NP, NP), to] = vale.astype(BF16)
            return carry

        lax.fori_loop(0, pts // width, products, 0)

    inside = min(bits, tiles - 1)

    def project(t, carry):
        for s in range(inside):
            @pl.when(t == s + 1)
            def _(s=s):
                pick_step(s)
        load_tile(t).wait()
        at = pl.ds(pl.multiple_of(t * TILE, TILE), TILE)
        waves[:, at] = dot(points[...], weights[t]).astype(BF16)
        return carry

    lax.fori_loop(0, tiles, project, 0)
    for s in range(inside, bits):
        pick_step(s)

    screen = pick[0].astype(F32)
    screen = jnp.concatenate([screen[:8], screen[8:]], axis=1)
    weighted_x = (waves[:NP].astype(F32) * bare[...]).astype(BF16)
    ex_t = dot_t(waves[:steps * NP], weighted_x)

    quarter = sbuf.shape[1]
    rep_rows = NV * quarter
    r, c = iota((rep_rows, NP), 0), iota((rep_rows, NP), 1)
    r_v2, r_v, r_ch = r // quarter, (r % quarter) // 4, r % 4
    rep_own, rep_mir = onehot(c == r_v2 * NV + r_v), onehot(c == r_v * NV + r_v2)
    keep_own, keep_mir = (c // 8) // 2 == r_ch, (c % 8) // 2 == r_ch
    r, c = iota((NP, 128), 0), iota((NP, 128), 1)
    c_cl, c_v2, c_c2 = c // 64, (c % 64) // 8, c % 8
    fit_own = ((r // 8) % 2 == c_cl) & (r % 8 == c_c2)
    fit_mir = (r % 2 == c_cl) & (r // 8 == c_c2)
    place = [onehot(c == r + 64 * cl) for cl in range(2)]
    r, c = iota((quarter, NP), 0), iota((quarter, NP), 1)
    rows_of = [onehot(c == (r // 4) * 8 + (r % 4) * 2 + cl) for cl in range(2)]

    own_x, mir_x = [], []
    for d in range(steps):
        base = (steps + 2 * d) * NP
        cond = waves[base:base + NP].astype(F32)
        vale = waves[base + NP:base + 2 * NP]
        row = max(2 * d - 1, 0)
        term = dot_t(vale, (cond * screen[row:row + 1]).astype(BF16)).astype(BF16)
        own_x.append(jnp.where(keep_own, dot(rep_own, term), 0.0).astype(BF16))
        if d:
            term = dot_t(vale, (cond * screen[2 * d:2 * d + 1]).astype(BF16)).astype(BF16)
            mir_x.append(jnp.where(keep_mir, dot(rep_mir, term), 0.0).astype(BF16))

    def gathered(parts, fit):
        total = 0.0
        for v2 in range(NV):
            stacked = jnp.concatenate([x[v2 * quarter:(v2 + 1) * quarter] for x in parts], axis=0)
            total = total + dot(stacked, onehot(fit & (c_v2 == v2)))
        return total

    direct = [gathered(own_x, fit_own), gathered(mir_x, fit_mir)]
    for e in range(2 * RSTEPS + 1):
        d = e if e < steps else e - RSTEPS
        exch = ex_t[d * NP:(d + 1) * NP].astype(BF16)
        pick_rows = dot_t if e < steps else dot
        spread = sum(dot(pick_rows(rows_of[cl], exch).astype(BF16), place[cl]) for cl in range(2))
        at = (e if e < steps else e - steps) * quarter
        sbuf[e] = 2.0 * spread - direct[e // steps][at:at + quarter]

    def own_rows(gg):
        return pl.ds(pl.multiple_of(gg * share, share), share)

    def final_copy(d, j, gg):
        to = ga(g + j)
        entries = pl.ds(RSTEPS + d, 1) if d else pl.ds(0, steps)
        return remote(
            sbuf.at[entries, own_rows(to)], rbuf.at[gg, entries],
            fsend.at[d, j], frecv.at[d, j], ka(k - d), to,
        )

    for d, j in moves:
        final_copy(d, j, g).start()
    for d, j in moves:
        final_copy(d, j, ga(g - j)).wait_recv()
    scale = NG ** (-0.5)
    for d in range(steps):
        total = sbuf[d, own_rows(g)]
        for j in range(1, n_ga):
            total = total + rbuf[ga(g - j), d]
        out[pl.ds((RSTEPS + d) * share, share)] = total * scale
        if d:
            total = rbuf[g, RSTEPS + d]
            for j in range(1, n_ga):
                total = total + rbuf[ga(g - j), RSTEPS + d]
            out[pl.ds((RSTEPS - d) * share, share)] = total * scale

    for d, j in moves:
        final_copy(d, j, g).wait_send()
        orb_copy(d, j, g).wait_send()
    for j in range(1, n_ka):
        kpt_copy(j, k).wait_send()
    for s in range(bits):
        pick_copy(s).wait_send()


def per_device(n_ka, n_ga, orbitals, interp_vectors, screening, bare_coulomb, slab_kpoints):
    _, bands, half_pts = orbitals.shape
    pts, cols = interp_vectors.shape
    steps = RSTEPS + 1
    entries = 2 * RSTEPS + 1
    rows = 3 * steps * NP
    quarter = NP * NP // 128
    share = quarter // n_ga
    tiles = cols // TILE
    bits = n_ka.bit_length() - 1
    dma = pltpu.SemaphoreType.DMA
    vmem = pl.BlockSpec(memory_space=pltpu.VMEM)
    hbm = pl.BlockSpec(memory_space=pl.ANY)
    result = pl.pallas_call(
        functools.partial(kernel, n_ka, n_ga),
        out_shape=jax.ShapeDtypeStruct((entries * share, 128), F32),
        in_specs=[vmem, pl.BlockSpec(memory_space=pltpu.SMEM), vmem, hbm, hbm],
        out_specs=vmem,
        scratch_shapes=[
            pltpu.VMEM((steps, n_ga, bands, half_pts), BF16),
            pltpu.VMEM((n_ka, 2, 8, 128), I32),
            pltpu.VMEM(screening.shape, BF16),
            pltpu.VMEM((n_ka, 16, cols // 2), BF16),
            pltpu.VMEM((n_ka, 16, cols // 2), BF16),
            pltpu.VMEM((rows, pts), BF16),
            pltpu.VMEM((tiles, pts, TILE), BF16),
            pltpu.VMEM((rows, cols), BF16),
            pltpu.VMEM((entries, quarter, 128), F32),
            pltpu.VMEM((n_ga, entries, share, 128), F32),
            dma((steps, n_ga)), dma((steps, n_ga)),
            dma((n_ka,)), dma((n_ka,)),
            dma((1,)), dma((tiles,)),
            dma((bits,)), dma((bits,)),
            dma((steps, n_ga)), dma((steps, n_ga)),
        ],
        compiler_params=pltpu.CompilerParams(
            collective_id=0, has_side_effects=True, vmem_limit_bytes=56 * 2 ** 20
        ),
        cost_estimate=pl.CostEstimate(
            flops=2 * rows * pts * cols, bytes_accessed=2 * pts * cols, transcendentals=0
        ),
    )(orbitals, slab_kpoints, bare_coulomb.reshape(1, -1), interp_vectors, screening)
    return result.reshape(1, entries, 1, share * 128)


def solution(mesh):
    in_specs = (P("ka", None, "ga"), P(None, "ga"), P("ka", "ga"), P("ga"), P("ka"))
    out_specs = P("ka", None, None, "ga")
    return jax.shard_map(
        functools.partial(per_device, mesh.shape["ka"], mesh.shape["ga"]),
        mesh=mesh, in_specs=in_specs, out_specs=out_specs, check_vma=False,
    )
```

```python
import functools

import jax
import jax.numpy as jnp
from jax import lax
from jax.experimental import pallas as pl
from jax.experimental.pallas import tpu as pltpu
from jax.sharding import PartitionSpec as P

NV = 8
NC = 8
NG = 4096
NKX = 96
RSTEPS = 3
NP = NV * NC
TILE = 256
F32, BF16, I32 = jnp.float32, jnp.bfloat16, jnp.int32


def dot(a, b):
    return lax.dot_general(a, b, (((1,), (0,)), ((), ())), preferred_element_type=F32)


def dot_t(a, b):
    return lax.dot_general(a, b, (((1,), (1,)), ((), ())), preferred_element_type=F32)


def iota(shape, dim):
    return lax.broadcasted_iota(I32, shape, dim)


def reverse(i, bits):
    return sum(((i >> s) & 1) << (bits - 1 - s) for s in range(bits))


def onehot(cond):
    return jnp.where(cond, 1.0, 0.0).astype(BF16)


def kernel(
    n_ka, n_ga,
    orb, kpt, bare, interp, screening, out,
    slots, kall, table, pick, arrived, points, weights, waves, sbuf, rbuf,
    osend, orecv, ksend, krecv, tsem, isem, psend, precv, fsend, frecv,
):
    k, g = lax.axis_index("ka"), lax.axis_index("ga")
    bits = n_ka.bit_length() - 1
    steps = RSTEPS + 1
    half_pts = orb.shape[2]
    pts, cols = interp.shape
    tiles = cols // TILE
    rows_here = screening.shape[0]
    share = sbuf.shape[1] // n_ga

    swaps = [(1 << s) * (1 - 2 * lax.rem(lax.div(k, 1 << s), 2)) for s in range(bits)]
    flips = [sum([swaps[s] for s in range(bits) if (j >> s) & 1], k) for j in range(n_ka)]

    def ka(x):
        return lax.rem(x + n_ka, n_ka)

    def ga(x):
        return lax.rem(x + n_ga, n_ga)

    def remote(src, dst, ss, rs, kk, gg):
        return pltpu.make_async_remote_copy(
            src_ref=src, dst_ref=dst, send_sem=ss, recv_sem=rs,
            device_id=(kk, gg), device_id_type=pl.DeviceIdType.MESH,
        )

    def load_tile(t):
        at = pl.ds(pl.multiple_of(t * TILE, TILE), TILE)
        return pltpu.make_async_copy(interp.at[:, at], weights.at[t], isem.at[t])

    barrier = pltpu.get_barrier_semaphore()
    peers = [(flips[j], g) for j in range(1, n_ka)]
    peers += [(ka(k + d), ga(g + j)) for d in range(-RSTEPS, RSTEPS + 1) for j in range(1, n_ga)]
    for kk, gg in peers:
        pl.semaphore_signal(barrier, inc=1, device_id=(kk, gg), device_id_type=pl.DeviceIdType.MESH)
    table_copy = pltpu.make_async_copy(screening, table, tsem.at[0])
    table_copy.start()
    for t in range(tiles):
        load_tile(t).start()
    point = kpt[0]
    kall[k, 0:1] = jnp.full((1, 128), lax.div(point, NKX), I32)
    kall[k, 1:2] = jnp.full((1, 128), lax.rem(point, NKX), I32)
    slots[0, g] = orb[0]
    pl.semaphore_wait(barrier, len(peers))

    def kpt_copy(j, owner):
        return remote(kall.at[owner], kall.at[owner], ksend.at[j], krecv.at[j], flips[j], g)

    moves = [(d, j) for d in range(steps) for j in range(n_ga) if d or j]

    def orb_copy(d, j, gg):
        return remote(
            orb.at[0], slots.at[d, gg], osend.at[d, j], orecv.at[d, j], ka(k + d), ga(g + j)
        )

    head = [m for m in moves if m[0] == 0]
    for d, j in head:
        orb_copy(d, j, g).start()
    for j in range(1, n_ka):
        kpt_copy(j, k).start()
    for d, j in moves[len(head):]:
        orb_copy(d, j, g).start()

    first = 3 * NP

    def ex_at(d):
        return first + (d - 1) * NP if d else 0

    def pair_at(d):
        return first + RSTEPS * NP + (d - 1) * 2 * NP if d else NP

    width = 512

    def products_of(d):
        for j in range(n_ga):
            if d or j:
                orb_copy(d, j, ga(g - j)).wait_recv()

        def products(c, carry):
            h, off = lax.div(c, half_pts // width), lax.rem(c, half_pts // width)
            at = pl.ds(pl.multiple_of(off * width, width), width)
            to = pl.ds(pl.multiple_of(c * width, width), width)
            own = slots[0, h, :, at].astype(F32)
            par = slots[d, h, :, at].astype(F32)
            own_v, own_c, par_v, par_c = own[:NV], own[NV:], par[:NV], par[NV:]
            ex = jnp.concatenate([par_v[i:i + 1] * par_c for i in range(NV)], axis=0)
            cond = jnp.concatenate([own_c[i:i + 1] * par_c for i in range(NC)], axis=0)
            vale = jnp.concatenate([par_v[i:i + 1] * own_v for i in range(NV)], axis=0)
            points[pl.ds(ex_at(d), NP), to] = ex.astype(BF16)
            points[pl.ds(pair_at(d), NP), to] = cond.astype(BF16)
            points[pl.ds(pair_at(d) + NP, NP), to] = vale.astype(BF16)
            return carry

        lax.fori_loop(0, pts // width, products, 0)

    def project_head(t, carry):
        load_tile(t).wait()
        at = pl.ds(pl.multiple_of(t * TILE, TILE), TILE)
        waves[:first, at] = dot(points[:first], weights[t]).astype(BF16)
        return carry

    products_of(0)
    lax.fori_loop(0, tiles, project_head, 0)

    for j in range(1, n_ka):
        kpt_copy(j, flips[j]).wait_recv()

    table_copy.wait()
    sub = iota((8, 128), 0)
    lane = iota((16, rows_here), 1)
    pieces = []
    for i in range(n_ka):
        dest = flips[reverse(i, bits)]
        dx, dy = kall[dest, 0:1], kall[dest, 1:2]
        want = jnp.zeros((8, 128), I32)
        for d in range(1, steps):
            other = ka(dest - d)
            x, y = dx - kall[other, 0:1], dy - kall[other, 1:2]
            there = jnp.where(x < 0, x + NKX, x) * NKX + jnp.where(y < 0, y + NKX, y)
            back = jnp.where(x > 0, NKX - x, -x) * NKX + jnp.where(y > 0, NKX - y, -y)
            want = jnp.where(sub == 2 * d - 1, there, want)
            want = jnp.where(sub == 2 * d, back, want)
        local = (want - k * rows_here)[:, :1]
        local = jnp.concatenate([local, local], axis=0)
        pieces.append(jnp.where(lane == local, 1.0, 0.0))
    picker = jnp.concatenate(pieces, axis=0).astype(BF16)
    half_cols = cols // 2
    picked = dot(picker, table[...])
    upper = iota((n_ka * 16, half_cols), 0) & 8
    picked = jnp.where(upper == 0, picked[:, :half_cols], picked[:, half_cols:])
    pick[...] = picked.astype(BF16).reshape(n_ka, 16, half_cols)

    def pick_copy(s):
        half = n_ka >> (s + 1)
        return remote(
            pick.at[pl.ds(half, half)], arrived.at[pl.ds(half, half)],
            psend.at[s], precv.at[s], flips[1 << s], g,
        )

    def pick_step(s):
        half = n_ka >> (s + 1)
        pick_copy(s).wait_recv()
        pick[:half] = (pick[:half].astype(F32) + arrived[half:2 * half].astype(F32)).astype(BF16)
        if s + 1 < bits:
            pick_copy(s + 1).start()

    pick_copy(0).start()

    for d in range(1, steps):
        products_of(d)

    inside = min(bits, tiles - 1)

    def project(t, carry):
        for s in range(inside):
            @pl.when(t == s + 1)
            def _(s=s):
                pick_step(s)
        at = pl.ds(pl.multiple_of(t * TILE, TILE), TILE)
        waves[first:, at] = dot(points[first:], weights[t]).astype(BF16)
        return carry

    lax.fori_loop(0, tiles, project, 0)
    for s in range(inside, bits):
        pick_step(s)

    screen = pick[0].astype(F32)
    screen = jnp.concatenate([screen[:8], screen[8:]], axis=1)
    weighted_x = (waves[:NP].astype(F32) * bare[...]).astype(BF16)
    ex_t = [dot_t(waves[ex_at(d):ex_at(d) + NP], weighted_x).astype(BF16) for d in range(steps)]

    quarter = sbuf.shape[1]
    rep_rows = NV * quarter
    r, c = iota((rep_rows, NP), 0), iota((rep_rows, NP), 1)
    r_v2, r_v, r_ch = r >> (quarter.bit_length() - 1), (r & (quarter - 1)) >> 2, r & 3
    rep_own, rep_mir = onehot(c == r_v2 * NV + r_v), onehot(c == r_v * NV + r_v2)
    keep_own, keep_mir = c >> 4 == r_ch, (c & 7) >> 1 == r_ch
    r, c = iota((NP, 128), 0), iota((NP, 128), 1)
    c_cl, c_v2, c_c2 = c >> 6, (c & 63) >> 3, c & 7
    fit_own = ((r >> 3) & 1 == c_cl) & (r & 7 == c_c2)
    fit_mir = (r & 1 == c_cl) & (r >> 3 == c_c2)
    place = [onehot(c == r + 64 * cl) for cl in range(2)]
    r, c = iota((quarter, NP), 0), iota((quarter, NP), 1)
    rows_of = [onehot(c == (r >> 2) * 8 + (r & 3) * 2 + cl) for cl in range(2)]

    own_x, mir_x = [], []
    for d in range(steps):
        base = pair_at(d)
        cond = waves[base:base + NP].astype(F32)
        vale = waves[base + NP:base + 2 * NP]
        row = max(2 * d - 1, 0)
        term = dot_t(vale, (cond * screen[row:row + 1]).astype(BF16)).astype(BF16)
        own_x.append(jnp.where(keep_own, dot(rep_own, term), 0.0).astype(BF16))
        if d:
            term = dot_t(vale, (cond * screen[2 * d:2 * d + 1]).astype(BF16)).astype(BF16)
            mir_x.append(jnp.where(keep_mir, dot(rep_mir, term), 0.0).astype(BF16))

    def gathered(parts, fit):
        total = 0.0
        for v2 in range(NV):
            stacked = jnp.concatenate([x[v2 * quarter:(v2 + 1) * quarter] for x in parts], axis=0)
            total = total + dot(stacked, onehot(fit & (c_v2 == v2)))
        return total

    direct = [gathered(own_x, fit_own), gathered(mir_x, fit_mir)]
    for e in range(2 * RSTEPS + 1):
        d = e if e < steps else e - RSTEPS
        exch = ex_t[d]
        pick_rows = dot_t if e < steps else dot
        spread = sum(dot(pick_rows(rows_of[cl], exch).astype(BF16), place[cl]) for cl in range(2))
        at = (e if e < steps else e - steps) * quarter
        sbuf[e] = 2.0 * spread - direct[e // steps][at:at + quarter]

    def own_rows(gg):
        return pl.ds(pl.multiple_of(gg * share, share), share)

    def final_copy(d, j, gg):
        to = ga(g + j)
        entries = pl.ds(RSTEPS + d, 1) if d else pl.ds(0, steps)
        return remote(
            sbuf.at[entries, own_rows(to)], rbuf.at[gg, entries],
            fsend.at[d, j], frecv.at[d, j], ka(k - d), to,
        )

    for d, j in moves:
        final_copy(d, j, g).start()
    for d, j in moves:
        final_copy(d, j, ga(g - j)).wait_recv()
    scale = NG ** (-0.5)
    for d in range(steps):
        total = sbuf[d, own_rows(g)]
        for j in range(1, n_ga):
            total = total + rbuf[ga(g - j), d]
        out[pl.ds((RSTEPS + d) * share, share)] = total * scale
        if d:
            total = rbuf[g, RSTEPS + d]
            for j in range(1, n_ga):
                total = total + rbuf[ga(g - j), RSTEPS + d]
            out[pl.ds((RSTEPS - d) * share, share)] = total * scale

    for d, j in moves:
        final_copy(d, j, g).wait_send()
        orb_copy(d, j, g).wait_send()
    for j in range(1, n_ka):
        kpt_copy(j, k).wait_send()
    for s in range(bits):
        pick_copy(s).wait_send()


def per_device(n_ka, n_ga, orbitals, interp_vectors, screening, bare_coulomb, slab_kpoints):
    _, bands, half_pts = orbitals.shape
    pts, cols = interp_vectors.shape
    steps = RSTEPS + 1
    entries = 2 * RSTEPS + 1
    rows = 3 * steps * NP
    quarter = NP * NP // 128
    share = quarter // n_ga
    tiles = cols // TILE
    bits = n_ka.bit_length() - 1
    dma = pltpu.SemaphoreType.DMA
    vmem = pl.BlockSpec(memory_space=pltpu.VMEM)
    hbm = pl.BlockSpec(memory_space=pl.ANY)
    result = pl.pallas_call(
        functools.partial(kernel, n_ka, n_ga),
        out_shape=jax.ShapeDtypeStruct((entries * share, 128), F32),
        in_specs=[vmem, pl.BlockSpec(memory_space=pltpu.SMEM), vmem, hbm, hbm],
        out_specs=vmem,
        scratch_shapes=[
            pltpu.VMEM((steps, n_ga, bands, half_pts), BF16),
            pltpu.VMEM((n_ka, 2, 128), I32),
            pltpu.VMEM(screening.shape, BF16),
            pltpu.VMEM((n_ka, 16, cols // 2), BF16),
            pltpu.VMEM((n_ka, 16, cols // 2), BF16),
            pltpu.VMEM((rows, pts), BF16),
            pltpu.VMEM((tiles, pts, TILE), BF16),
            pltpu.VMEM((rows, cols), BF16),
            pltpu.VMEM((entries, quarter, 128), F32),
            pltpu.VMEM((n_ga, entries, share, 128), F32),
            dma((steps, n_ga)), dma((steps, n_ga)),
            dma((n_ka,)), dma((n_ka,)),
            dma((1,)), dma((tiles,)),
            dma((bits,)), dma((bits,)),
            dma((steps, n_ga)), dma((steps, n_ga)),
        ],
        compiler_params=pltpu.CompilerParams(
            collective_id=0, has_side_effects=True, vmem_limit_bytes=56 * 2 ** 20
        ),
        cost_estimate=pl.CostEstimate(
            flops=2 * rows * pts * cols, bytes_accessed=2 * pts * cols, transcendentals=0
        ),
    )(orbitals, slab_kpoints, bare_coulomb.reshape(1, -1), interp_vectors, screening)
    return result.reshape(1, entries, 1, share * 128)


def solution(mesh):
    in_specs = (P("ka", None, "ga"), P(None, "ga"), P("ka", "ga"), P("ga"), P("ka"))
    out_specs = P("ka", None, None, "ga")
    return jax.shard_map(
        functools.partial(per_device, mesh.shape["ka"], mesh.shape["ga"]),
        mesh=mesh, in_specs=in_specs, out_specs=out_specs, check_vma=False,
    )
```

```python
import functools

import jax
import jax.numpy as jnp
from jax import lax
from jax.experimental import pallas as pl
from jax.experimental.pallas import tpu as pltpu
from jax.sharding import PartitionSpec as P

NV = 8
NC = 8
NG = 4096
NKX = 96
RSTEPS = 3
NP = NV * NC
TILE = 512
F32, BF16, I32 = jnp.float32, jnp.bfloat16, jnp.int32


def dot(a, b):
    return lax.dot_general(a, b, (((1,), (0,)), ((), ())), preferred_element_type=F32)


def dot_t(a, b):
    return lax.dot_general(a, b, (((1,), (1,)), ((), ())), preferred_element_type=F32)


def iota(shape, dim):
    return lax.broadcasted_iota(I32, shape, dim)


def reverse(i, bits):
    return sum(((i >> s) & 1) << (bits - 1 - s) for s in range(bits))


def onehot(cond):
    return jnp.where(cond, 1.0, 0.0).astype(BF16)


def kernel(
    n_ka, n_ga,
    orb, kpt, bare, interp, screening, out,
    slots, kall, table, pick, arrived, points, weights, waves, sbuf, rbuf,
    osend, orecv, ksend, krecv, tsem, isem, psend, precv, fsend, frecv,
):
    k, g = lax.axis_index("ka"), lax.axis_index("ga")
    bits = n_ka.bit_length() - 1
    steps = RSTEPS + 1
    half_pts = orb.shape[2]
    pts, cols = interp.shape
    tiles = cols // TILE
    rows_here = screening.shape[0]
    share = sbuf.shape[1] // n_ga

    swaps = [(1 << s) * (1 - 2 * lax.rem(lax.div(k, 1 << s), 2)) for s in range(bits)]
    flips = [sum([swaps[s] for s in range(bits) if (j >> s) & 1], k) for j in range(n_ka)]

    def ka(x):
        return lax.rem(x + n_ka, n_ka)

    def ga(x):
        return lax.rem(x + n_ga, n_ga)

    def remote(src, dst, ss, rs, kk, gg):
        return pltpu.make_async_remote_copy(
            src_ref=src, dst_ref=dst, send_sem=ss, recv_sem=rs,
            device_id=(kk, gg), device_id_type=pl.DeviceIdType.MESH,
        )

    def load_tile(t):
        at = pl.ds(pl.multiple_of(t * TILE, TILE), TILE)
        return pltpu.make_async_copy(interp.at[:, at], weights.at[t], isem.at[t])

    barrier = pltpu.get_barrier_semaphore()
    peers = [(flips[j], g) for j in range(1, n_ka)]
    peers += [(ka(k + d), ga(g + j)) for d in range(-RSTEPS, RSTEPS + 1) for j in range(1, n_ga)]
    for kk, gg in peers:
        pl.semaphore_signal(barrier, inc=1, device_id=(kk, gg), device_id_type=pl.DeviceIdType.MESH)
    table_copy = pltpu.make_async_copy(screening, table, tsem.at[0])
    table_copy.start()
    for t in range(tiles):
        load_tile(t).start()
    point = kpt[0]
    kall[k, 0:1] = jnp.full((1, 128), lax.div(point, NKX), I32)
    kall[k, 1:2] = jnp.full((1, 128), lax.rem(point, NKX), I32)
    slots[0, g] = orb[0]
    pl.semaphore_wait(barrier, len(peers))

    def kpt_copy(j, owner):
        return remote(kall.at[owner], kall.at[owner], ksend.at[j], krecv.at[j], flips[j], g)

    moves = [(d, j) for d in range(steps) for j in range(n_ga) if d or j]

    def orb_copy(d, j, gg):
        return remote(
            orb.at[0], slots.at[d, gg], osend.at[d, j], orecv.at[d, j], ka(k + d), ga(g + j)
        )

    head = [m for m in moves if m[0] == 0]
    for d, j in head:
        orb_copy(d, j, g).start()
    for j in range(1, n_ka):
        kpt_copy(j, k).start()
    for d, j in moves[len(head):]:
        orb_copy(d, j, g).start()

    first = 3 * NP

    def ex_at(d):
        return first + (d - 1) * NP if d else 0

    def pair_at(d):
        return first + RSTEPS * NP + (d - 1) * 2 * NP if d else NP

    width = 512

    def products_of(d):
        for j in range(n_ga):
            if d or j:
                orb_copy(d, j, ga(g - j)).wait_recv()

        def products(c, carry):
            h, off = lax.div(c, half_pts // width), lax.rem(c, half_pts // width)
            at = pl.ds(pl.multiple_of(off * width, width), width)
            to = pl.ds(pl.multiple_of(c * width, width), width)
            own = slots[0, h, :, at].astype(F32)
            par = slots[d, h, :, at].astype(F32)
            own_v, own_c, par_v, par_c = own[:NV], own[NV:], par[:NV], par[NV:]
            ex = jnp.concatenate([par_v[i:i + 1] * par_c for i in range(NV)], axis=0)
            cond = jnp.concatenate([own_c[i:i + 1] * par_c for i in range(NC)], axis=0)
            vale = jnp.concatenate([par_v[i:i + 1] * own_v for i in range(NV)], axis=0)
            points[pl.ds(ex_at(d), NP), to] = ex.astype(BF16)
            points[pl.ds(pair_at(d), NP), to] = cond.astype(BF16)
            points[pl.ds(pair_at(d) + NP, NP), to] = vale.astype(BF16)
            return carry

        lax.fori_loop(0, pts // width, products, 0)

    def project_head(t, carry):
        load_tile(t).wait()
        at = pl.ds(pl.multiple_of(t * TILE, TILE), TILE)
        waves[:first, at] = dot(points[:first], weights[t]).astype(BF16)
        return carry

    products_of(0)
    lax.fori_loop(0, tiles, project_head, 0)

    for j in range(1, n_ka):
        kpt_copy(j, flips[j]).wait_recv()

    table_copy.wait()
    sub = iota((8, 128), 0)
    lane = iota((16, rows_here), 1)
    pieces = []
    for i in range(n_ka):
        dest = flips[reverse(i, bits)]
        dx, dy = kall[dest, 0:1], kall[dest, 1:2]
        want = jnp.zeros((8, 128), I32)
        for d in range(1, steps):
            other = ka(dest - d)
            x, y = dx - kall[other, 0:1], dy - kall[other, 1:2]
            there = jnp.where(x < 0, x + NKX, x) * NKX + jnp.where(y < 0, y + NKX, y)
            back = jnp.where(x > 0, NKX - x, -x) * NKX + jnp.where(y > 0, NKX - y, -y)
            want = jnp.where(sub == 2 * d - 1, there, want)
            want = jnp.where(sub == 2 * d, back, want)
        local = (want - k * rows_here)[:, :1]
        local = jnp.concatenate([local, local], axis=0)
        pieces.append(jnp.where(lane == local, 1.0, 0.0))
    picker = jnp.concatenate(pieces, axis=0).astype(BF16)
    half_cols = cols // 2
    picked = dot(picker, table[...])
    upper = iota((n_ka * 16, half_cols), 0) & 8
    picked = jnp.where(upper == 0, picked[:, :half_cols], picked[:, half_cols:])
    pick[...] = picked.astype(BF16).reshape(n_ka, 16, half_cols)

    def pick_copy(s):
        half = n_ka >> (s + 1)
        return remote(
            pick.at[pl.ds(half, half)], arrived.at[pl.ds(half, half)],
            psend.at[s], precv.at[s], flips[1 << s], g,
        )

    def pick_step(s):
        half = n_ka >> (s + 1)
        pick_copy(s).wait_recv()
        pick[:half] = (pick[:half].astype(F32) + arrived[half:2 * half].astype(F32)).astype(BF16)
        if s + 1 < bits:
            pick_copy(s + 1).start()

    pick_copy(0).start()

    for d in range(1, steps):
        products_of(d)

    inside = min(bits, tiles)

    def project(t, carry):
        for s in range(inside):
            @pl.when(t == s)
            def _(s=s):
                pick_step(s)
        at = pl.ds(pl.multiple_of(t * TILE, TILE), TILE)
        waves[first:, at] = dot(points[first:], weights[t]).astype(BF16)
        return carry

    lax.fori_loop(0, tiles, project, 0)
    for s in range(inside, bits):
        pick_step(s)

    screen = pick[0].astype(F32)
    screen = jnp.concatenate([screen[:8], screen[8:]], axis=1)
    weighted_x = (waves[:NP].astype(F32) * bare[...]).astype(BF16)
    ex_t = [dot_t(waves[ex_at(d):ex_at(d) + NP], weighted_x).astype(BF16) for d in range(steps)]

    quarter = sbuf.shape[1]
    rep_rows = NV * quarter
    r, c = iota((rep_rows, NP), 0), iota((rep_rows, NP), 1)
    r_v2, r_v, r_ch = r >> (quarter.bit_length() - 1), (r & (quarter - 1)) >> 2, r & 3
    rep_own, rep_mir = onehot(c == r_v2 * NV + r_v), onehot(c == r_v * NV + r_v2)
    keep_own, keep_mir = c >> 4 == r_ch, (c & 7) >> 1 == r_ch
    r, c = iota((NP, 128), 0), iota((NP, 128), 1)
    c_cl, c_v2, c_c2 = c >> 6, (c & 63) >> 3, c & 7
    fit_own = ((r >> 3) & 1 == c_cl) & (r & 7 == c_c2)
    fit_mir = (r & 1 == c_cl) & (r >> 3 == c_c2)
    place = [onehot(c == r + 64 * cl) for cl in range(2)]
    r, c = iota((quarter, NP), 0), iota((quarter, NP), 1)
    rows_of = [onehot(c == (r >> 2) * 8 + (r & 3) * 2 + cl) for cl in range(2)]

    own_x, mir_x = [], []
    for d in range(steps):
        base = pair_at(d)
        cond = waves[base:base + NP].astype(F32)
        vale = waves[base + NP:base + 2 * NP]
        row = max(2 * d - 1, 0)
        term = dot_t(vale, (cond * screen[row:row + 1]).astype(BF16)).astype(BF16)
        own_x.append(jnp.where(keep_own, dot(rep_own, term), 0.0).astype(BF16))
        if d:
            term = dot_t(vale, (cond * screen[2 * d:2 * d + 1]).astype(BF16)).astype(BF16)
            mir_x.append(jnp.where(keep_mir, dot(rep_mir, term), 0.0).astype(BF16))

    def gathered(parts, fit):
        total = 0.0
        for v2 in range(NV):
            stacked = jnp.concatenate([x[v2 * quarter:(v2 + 1) * quarter] for x in parts], axis=0)
            total = total + dot(stacked, onehot(fit & (c_v2 == v2)))
        return total

    direct = [gathered(own_x, fit_own), gathered(mir_x, fit_mir)]
    for e in range(2 * RSTEPS + 1):
        d = e if e < steps else e - RSTEPS
        exch = ex_t[d]
        pick_rows = dot_t if e < steps else dot
        spread = sum(dot(pick_rows(rows_of[cl], exch).astype(BF16), place[cl]) for cl in range(2))
        at = (e if e < steps else e - steps) * quarter
        sbuf[e] = 2.0 * spread - direct[e // steps][at:at + quarter]

    def own_rows(gg):
        return pl.ds(pl.multiple_of(gg * share, share), share)

    def final_copy(d, j, gg):
        to = ga(g + j)
        entries = pl.ds(RSTEPS + d, 1) if d else pl.ds(0, steps)
        return remote(
            sbuf.at[entries, own_rows(to)], rbuf.at[gg, entries],
            fsend.at[d, j], frecv.at[d, j], ka(k - d), to,
        )

    for d, j in moves:
        final_copy(d, j, g).start()
    for d, j in moves:
        final_copy(d, j, ga(g - j)).wait_recv()
    scale = NG ** (-0.5)
    for d in range(steps):
        total = sbuf[d, own_rows(g)]
        for j in range(1, n_ga):
            total = total + rbuf[ga(g - j), d]
        out[pl.ds((RSTEPS + d) * share, share)] = total * scale
        if d:
            total = rbuf[g, RSTEPS + d]
            for j in range(1, n_ga):
                total = total + rbuf[ga(g - j), RSTEPS + d]
            out[pl.ds((RSTEPS - d) * share, share)] = total * scale

    for d, j in moves:
        final_copy(d, j, g).wait_send()
        orb_copy(d, j, g).wait_send()
    for j in range(1, n_ka):
        kpt_copy(j, k).wait_send()
    for s in range(bits):
        pick_copy(s).wait_send()


def per_device(n_ka, n_ga, orbitals, interp_vectors, screening, bare_coulomb, slab_kpoints):
    _, bands, half_pts = orbitals.shape
    pts, cols = interp_vectors.shape
    steps = RSTEPS + 1
    entries = 2 * RSTEPS + 1
    rows = 3 * steps * NP
    quarter = NP * NP // 128
    share = quarter // n_ga
    tiles = cols // TILE
    bits = n_ka.bit_length() - 1
    dma = pltpu.SemaphoreType.DMA
    vmem = pl.BlockSpec(memory_space=pltpu.VMEM)
    hbm = pl.BlockSpec(memory_space=pl.ANY)
    result = pl.pallas_call(
        functools.partial(kernel, n_ka, n_ga),
        out_shape=jax.ShapeDtypeStruct((entries * share, 128), F32),
        in_specs=[vmem, pl.BlockSpec(memory_space=pltpu.SMEM), vmem, hbm, hbm],
        out_specs=vmem,
        scratch_shapes=[
            pltpu.VMEM((steps, n_ga, bands, half_pts), BF16),
            pltpu.VMEM((n_ka, 2, 128), I32),
            pltpu.VMEM(screening.shape, BF16),
            pltpu.VMEM((n_ka, 16, cols // 2), BF16),
            pltpu.VMEM((n_ka, 16, cols // 2), BF16),
            pltpu.VMEM((rows, pts), BF16),
            pltpu.VMEM((tiles, pts, TILE), BF16),
            pltpu.VMEM((rows, cols), BF16),
            pltpu.VMEM((entries, quarter, 128), F32),
            pltpu.VMEM((n_ga, entries, share, 128), F32),
            dma((steps, n_ga)), dma((steps, n_ga)),
            dma((n_ka,)), dma((n_ka,)),
            dma((1,)), dma((tiles,)),
            dma((bits,)), dma((bits,)),
            dma((steps, n_ga)), dma((steps, n_ga)),
        ],
        compiler_params=pltpu.CompilerParams(
            collective_id=0, has_side_effects=True, vmem_limit_bytes=56 * 2 ** 20
        ),
        cost_estimate=pl.CostEstimate(
            flops=2 * rows * pts * cols, bytes_accessed=2 * pts * cols, transcendentals=0
        ),
    )(orbitals, slab_kpoints, bare_coulomb.reshape(1, -1), interp_vectors, screening)
    return result.reshape(1, entries, 1, share * 128)


def solution(mesh):
    in_specs = (P("ka", None, "ga"), P(None, "ga"), P("ka", "ga"), P("ga"), P("ka"))
    out_specs = P("ka", None, None, "ga")
    return jax.shard_map(
        functools.partial(per_device, mesh.shape["ka"], mesh.shape["ga"]),
        mesh=mesh, in_specs=in_specs, out_specs=out_specs, check_vma=False,
    )
```
